32 devices in a mesh: dp: 4 (over z), vocab: 8 (over y, x, core).
Axes of the slice: x: 2, y: 2, z: 4, core: 2. Of those that a mesh axis runs over, the one named last changes fastest.
Arguments:
- hidden: bfloat16 [4, 2, 64, 4608], P('dp'), may hold values from -6 to 6
- table: bfloat16 [18432, 4608], P('vocab', 'dp'), may hold values from -0.25 to 0.25
- new_mask: int32 [18432], P('vocab'), may hold values from 0 to 1, as said below
- labels: int32 [4, 2, 64], P('dp'), may hold values from 0 to 18431
- in_grad: bfloat16 [4, 2, 192, 4608], P('dp', None, 'vocab'), may hold values from -0.75 to 0.75
- item_owner: int32 [4, 2, 192, 1], P('dp', None, 'vocab'), may hold values from 0 to 7; in each aligned block of 24 rows (0 to 23, 24 to 47, ..., all dimensions but the last counted through in order) at most 6 rows name the same one
- item_slot: int32 [4, 2, 192], P('dp', None, 'vocab'), may hold values from 0 to 255
- first_moment: float32 [2048, 4608], P('vocab', 'dp'), may hold values from -0.75 to 0.75
- second_moment: float32 [2048, 4608], P('vocab', 'dp'), may hold values from 0.0001 to 0.01
Outputs:
- token_loss: float32 [4, 2, 64], P('dp')
- d_hidden: bfloat16 [4, 2, 64, 4608], P('dp', None, None, 'vocab')
- update: float32 [2048, 4608], P('vocab', 'dp')
- first_out: float32 [2048, 4608], P('vocab', 'dp')
- second_out: float32 [2048, 4608], P('vocab', 'dp')
The draws below stay inside these ranges and needn't reach their ends.
Inputs may be any that keep to these rules, and one draw needn't show every extreme that they name: `new_mask`: each aligned block of 2304 entries holds exactly 256 ones. `item_owner`: within the 24 rows of one device in one block, no shard is named more than 6 times, a bound that some block reaches.
All inputs are finite; a program needn't handle non-finite values.
Results may differ from the reference program's by a relative error of at most 0.006.
Values may be sent and summed in bfloat16 or wider, within the bound.
A program may use at most 128 MiB of HBM per device.

```python
import math
import jax
import jax.numpy as jnp
import numpy as np
from jax import lax

D = 4608
VOCAB_DEV = 2304
NEW_DEV = 256
SPAN = 64
SPANS = 2
ITEMS_DEV = 24
CAP = 6
VOCAB = 18432
NEW_ROWS = 2048
ITEMS = 192
N_DP = 4
N_VOCAB = 8


def draw_new_mask(key, part):
    shards = VOCAB // VOCAB_DEV
    keys = jax.random.split(jax.random.fold_in(key, 17), shards)
    orders = jax.vmap(lambda single: jax.random.permutation(single, VOCAB_DEV))(keys)
    return (orders < NEW_DEV).astype(jnp.int32).reshape(-1)


def plant(array, key, least, largest):
    spot = [jax.random.randint(jax.random.fold_in(key, axis), (), 0, length) for axis, length in enumerate(array.shape)]
    widest = array.shape.index(max(array.shape))
    next_to = spot[:widest] + [(spot[widest] + 1) % array.shape[widest]] + spot[widest + 1:]
    return array.at[tuple(spot)].set(least).at[tuple(next_to)].set(largest)


def steps_of(stream_key, extent, cuts, smallest, largest):
    level, own = 1.0, jax.random.fold_in(stream_key, 6)
    for position, blocks in cuts:
        steps = jnp.exp(jax.random.uniform(jax.random.fold_in(own, position), (blocks,), jnp.float32, smallest / len(cuts), largest / len(cuts)))
        level = level * jnp.repeat(steps, extent[position] // blocks).reshape([-1 if axis == position else 1 for axis in range(len(extent))])
    return level


def rank_bounds(count, skew):
    loads = [(1 << 20) // math.isqrt(grade ** skew) + 1 for grade in range(1, count + 1)]
    width = 1 + sum(loads) // (1 << 30)
    return np.cumsum(np.array([max(1, weight // width) for weight in loads]))


def ranked_ids(stream_key, dims, count, slope):
    table = rank_bounds(count, slope)
    pick = jax.random.randint(jax.random.fold_in(stream_key, 1), dims, 0, int(table[count - 1]))
    standing = jnp.searchsorted(jnp.asarray(table, jnp.int32), pick, side="right")
    return jax.random.permutation(jax.random.fold_in(stream_key, 2), count)[standing].astype(jnp.int32)


def assign_block(rng, own, number, rows, number_of, top, limit, lean):
    order = jax.random.permutation(rng, number_of)
    packed, usual = shares(number_of, rows * top, limit, lean, True), shares(number_of, rows * top, limit, lean, False)
    places = jnp.arange(number_of)

    def named(sizes, offset_by):
        used = int((sizes > 0).sum())
        fixed = max(1, used // 4)
        passed = fixed + (places - fixed + offset_by * (used - fixed)) % max(1, number_of - fixed)
        return jnp.zeros((number_of,), jnp.int32).at[order[jnp.where(places < fixed, places, passed)]].set(jnp.asarray(sizes, jnp.int32))

    sizes = jnp.where(number % 4 == 0, named(packed, number // 4), named(usual, number - number // 4 - 1))
    mixed = jax.random.permutation(jax.random.fold_in(own, 3), number_of)
    giver, receiver = mixed[0:number_of // 2 * 2:2], mixed[1:number_of // 2 * 2:2]
    slack = jnp.minimum(sizes[giver] - 1, limit - sizes[receiver]) // 2
    slack = jnp.where((giver == order[0]) | (receiver == order[0]) | (sizes[receiver] == 0), 0, jnp.maximum(slack, 0))
    passed = jax.random.randint(jax.random.fold_in(own, 4), (number_of // 2,), 0, 1 << 20) % (slack + 1)
    sizes = sizes.at[giver].add(-passed).at[receiver].add(passed)
    items = jnp.searchsorted(jnp.cumsum(sizes), jnp.arange(rows * top), side="right").astype(jnp.int32)
    grid = items.reshape(top, rows).T
    grid = grid[jax.random.permutation(jax.random.fold_in(own, 1), rows)]
    offset_by = jax.random.randint(jax.random.fold_in(own, 2), (rows, 1), 0, top)
    return jnp.take_along_axis(grid, (jnp.arange(top)[None, :] + offset_by) % top, axis=1)


def shares(amount, total, most, skew, full):
    loads = [(1 << 20) // math.isqrt(grade ** skew) + 1 for grade in range(1, amount + 1)]
    largest = most if full else min(most, max(-(-total // amount), total * loads[0] // sum(loads)))
    least = 1 if total - largest >= amount - 1 else 0
    holding, spare = [largest] + [least] * (amount - 1), total - largest - least * (amount - 1)
    while spare > 0:
        movable = [i for i in range(1, amount) if holding[i] < largest] or [i for i in range(1, amount) if holding[i] < most]
        whole, left = sum([loads[i] for i in movable]), spare
        for i in movable:
            more = min(most - holding[i], max(1, left * loads[i] // whole), spare)
            holding[i] = holding[i] + more
            spare = spare - more
    return np.array(holding)


def bell_draw(own_key, shape, width, limit, cuts=(), kind=jnp.bfloat16):
    level = steps_of(own_key, shape, cuts, -0.22, 0.18) if cuts else 1.0
    array = jax.random.normal(own_key, shape, jnp.float32) * width * level
    return jnp.minimum(jnp.maximum(array, -limit), limit).astype(kind)


def setup_inputs(seed: int = 0) -> dict:
    streams_of = jax.random.split(jax.random.key(seed), 10)
    hidden = bell_draw(streams_of[0], (N_DP, SPANS, SPAN, D), 1.0, 6.0, ((0, 4),))
    table = bell_draw(streams_of[1], (VOCAB, D), (D // 9) ** -0.5, 0.25, ((0, 8), (1, 4)))
    new_mask = draw_new_mask(jax.random.fold_in(streams_of[9], 71), 0)
    labels = plant(ranked_ids(streams_of[3], (N_DP, SPANS, SPAN), VOCAB, 2), jax.random.fold_in(streams_of[3], 3), 0, VOCAB - 1).astype(jnp.int32)
    in_grad = bell_draw(streams_of[4], (N_DP, SPANS, ITEMS, D), 0.05, 0.75, ((0, 4), (2, 8)))
    item_owner_keys = jax.random.split(jax.random.fold_in(streams_of[5], 1), N_DP * SPANS * ITEMS // ITEMS_DEV)
    item_owner_turns = jax.random.permutation(jax.random.fold_in(streams_of[5], 3), N_DP * SPANS * ITEMS // ITEMS_DEV)
    item_owner = jax.vmap(lambda own, number: assign_block(jax.random.fold_in(streams_of[5], 2), own, number, ITEMS_DEV, N_VOCAB, 1, CAP, 2))(item_owner_keys, item_owner_turns).reshape((N_DP, SPANS, ITEMS, 1))
    item_slot = plant(jax.random.randint(streams_of[6], (N_DP, SPANS, ITEMS), 0, NEW_DEV), jax.random.fold_in(streams_of[6], 1), 0, NEW_DEV - 1).astype(jnp.int32)
    first_moment = bell_draw(streams_of[7], (NEW_ROWS, D), 0.05, 0.75, ((0, 8), (1, 4)), jnp.float32)
    second_moment = jnp.clip(jnp.exp(math.log(0.01) - 4.6051702 * jax.random.uniform(streams_of[8], (NEW_ROWS, D), jnp.float32) ** steps_of(streams_of[8], (NEW_ROWS, D), ((0, 8), (1, 4)), -0.2, 0.2)), 0.0001, 0.01)
    return dict(hidden=hidden, table=table, new_mask=new_mask, labels=labels, in_grad=in_grad, item_owner=item_owner, item_slot=item_slot, first_moment=first_moment, second_moment=second_moment)


cap_value = 30.0
beta_one = 0.9
beta_two = 0.95
step_count = 10
epsilon = 1e-08
decay_rate = 0.1

def reference(hidden, table, new_mask, labels, in_grad, item_owner, item_slot, first_moment, second_moment):
    shards = new_mask.shape[0] // VOCAB_DEV
    order = jnp.argsort(1 - new_mask.reshape(shards, VOCAB_DEV), axis=1, stable=True)[:, :NEW_DEV].astype(jnp.int32)
    offsets = (jnp.arange(shards, dtype=jnp.int32) * VOCAB_DEV)[:, None]
    new_index = (order + offsets).reshape(-1).astype(jnp.int32)
    flat_hidden = hidden.reshape(-1, SPAN, D)
    flat_labels = labels.reshape(-1, SPAN)
    vocab_rows = table.shape[0]

    def one_block(carry, inputs):
        states, label_row = inputs
        raw = lax.dot_general(states, table, (((1,), (1,)), ((), ())), preferred_element_type=jnp.float32)
        capped = cap_value * jnp.tanh(raw / cap_value)
        expd = jnp.exp(capped)
        total = lax.optimization_barrier(jnp.sum(expd, axis=1))
        hits = jnp.arange(vocab_rows, dtype=jnp.int32)[None, :] == label_row[:, None]
        picked = lax.optimization_barrier(jnp.sum(jnp.where(hits, capped, 0.0), axis=1))
        loss = jnp.log(total) - picked
        error = ((expd / total[:, None] - hits.astype(jnp.float32)) * (1.0 - (capped / cap_value) ** 2)).astype(jnp.bfloat16)
        dstate = jnp.dot(error, table, preferred_element_type=jnp.float32).astype(jnp.bfloat16)
        chosen = error[:, new_index]
        carry = carry + jnp.dot(chosen.T, states, preferred_element_type=jnp.float32)
        return (carry, (loss, dstate))
    start = jnp.zeros((new_index.shape[0], D), jnp.float32)
    grads, (losses, dstates) = lax.scan(one_block, start, (flat_hidden, flat_labels))
    rows = in_grad.reshape(-1, D).astype(jnp.float32)
    targets = (item_owner.reshape(-1) * NEW_DEV + item_slot.reshape(-1)).astype(jnp.int32)
    grads = grads + jax.ops.segment_sum(rows, targets, num_segments=new_index.shape[0])
    params = table[new_index].astype(jnp.float32)
    first_out = beta_one * first_moment + (1.0 - beta_one) * grads
    second_out = beta_two * second_moment + (1.0 - beta_two) * grads * grads
    update = first_out / (1.0 - beta_one ** step_count) / (jnp.sqrt(second_out / (1.0 - beta_two ** step_count)) + epsilon) + decay_rate * params
    return (losses.reshape(labels.shape), dstates.reshape(hidden.shape), update, first_out, second_out)
```

```python
import jax
import jax.numpy as jnp
from jax import lax
from jax.sharding import PartitionSpec as P

cap_value = 30.0
beta_one = 0.9
beta_two = 0.95
step_count = 10
epsilon = 1e-08
decay_rate = 0.1


def select_rows(new_mask, new_count):
    ranked = jnp.cumsum(new_mask) - 1
    wanted = (ranked[None, :] == jnp.arange(new_count, dtype=jnp.int32)[:, None]) & (
        new_mask[None, :] == 1
    )
    return wanted.astype(jnp.bfloat16)


def softmax_error(raw, label_row, vocab_start):
    capped = cap_value * jnp.tanh(raw / cap_value)
    expd = jnp.exp(capped)
    hits = jnp.arange(raw.shape[1], dtype=jnp.int32)[None, :] + vocab_start == label_row[:, None]
    local_total = jnp.sum(expd, axis=1)
    local_pick = jnp.sum(jnp.where(hits, capped, 0.0), axis=1)
    total, picked = lax.psum(jnp.stack([local_total, local_pick]), "vocab")
    loss = jnp.log(total) - picked
    error = (
        (expd / total[:, None] - hits.astype(jnp.float32)) * (1.0 - (capped / cap_value) ** 2)
    ).astype(jnp.bfloat16)
    return (loss, error)


def gather_states(states, shards):
    share = states.shape[0] // shards
    mine = lax.dynamic_slice_in_dim(states, lax.axis_index("vocab") * share, share, 0)
    groups = lax.axis_size("dp")
    cut = lax.all_to_all(mine, "dp", split_axis=1, concat_axis=0, tiled=True)
    cut = cut.reshape(groups, share, -1)
    return lax.all_gather(cut, "vocab", axis=1, tiled=True).reshape(groups * share * shards, -1)


def finish_hidden(part, groups, shards):
    ratio = shards // groups
    mine = lax.psum_scatter(part.astype(jnp.bfloat16), "vocab", scatter_dimension=0, tiled=True)
    rows, columns = mine.shape
    pieces = mine.reshape(rows, ratio, columns // ratio).transpose(1, 0, 2)
    place = lax.rem(lax.axis_index("vocab"), ratio)
    got = []
    for r in range(ratio):
        pairs = [
            (d * shards + v, (v // ratio) * shards + ratio * d + (v % ratio + r) % ratio)
            for d in range(groups)
            for v in range(shards)
        ]
        piece = lax.dynamic_index_in_dim(pieces, lax.rem(place + r, ratio), 0, keepdims=False)
        got.append(lax.ppermute(piece, ("dp", "vocab"), pairs))
    order = lax.rem(place - jnp.arange(ratio, dtype=jnp.int32) + ratio, ratio)
    return jnp.stack(got)[order].reshape(ratio * rows, columns // ratio)


def pack_items(rows, owner, slot, shards, capacity, groups):
    onehot = (owner[:, None] == jnp.arange(shards, dtype=jnp.int32)[None, :]).astype(jnp.int32)
    running = jnp.cumsum(onehot, axis=0)
    ranked = jnp.sum(onehot * running, axis=1) - 1
    place = owner * capacity + ranked
    placing = jnp.arange(shards * capacity, dtype=jnp.int32)[:, None] == place[None, :]
    sent = jnp.dot(placing.astype(jnp.bfloat16), rows, preferred_element_type=jnp.float32).astype(
        jnp.bfloat16
    )
    targets = jnp.sum(placing.astype(jnp.int32) * (slot + 1)[None, :], axis=1)
    sent = sent.reshape(shards, capacity, groups, -1).transpose(2, 0, 1, 3)
    high, low = (targets // 128).astype(jnp.bfloat16), (targets % 128).astype(jnp.bfloat16)
    code = jnp.stack([high, low], axis=1).reshape(1, shards, capacity, 2)
    code = jnp.broadcast_to(jnp.pad(code, ((0, 0), (0, 0), (0, 0), (0, 126))), (groups, shards, capacity, 128))
    return jnp.concatenate([sent, code], axis=3)


def scatter_items(rows, targets, new_count):
    picking = (jnp.arange(new_count, dtype=jnp.int32)[:, None] == targets[None, :]).astype(
        jnp.bfloat16
    )
    return jnp.dot(picking, rows, preferred_element_type=jnp.float32)


def body(
    hidden, table, new_mask, labels, in_grad, item_owner, item_slot, first_moment, second_moment
):
    blocks, span, width = hidden.shape[1:]
    slice_width = table.shape[1]
    new_count = first_moment.shape[0]
    shards = lax.axis_size("vocab")
    groups = lax.axis_size("dp")
    items_here = in_grad.shape[2]
    capacity = max(2, (2 * items_here + shards - 1) // shards)
    vocab_start = lax.axis_index("vocab") * table.shape[0]
    spread = gather_states(hidden.reshape(blocks * span, width), shards)
    packed = jnp.concatenate(
        [
            pack_items(
                in_grad[0, c], item_owner[0, c, :, 0], item_slot[0, c], shards, capacity, groups
            )
            for c in range(blocks)
        ],
        axis=2,
    ).reshape(groups * shards, blocks * capacity, slice_width + 128)
    got = lax.all_to_all(packed, ("dp", "vocab"), split_axis=0, concat_axis=0, tiled=True)
    got = got.reshape(-1, slice_width + 128)
    targets = (
        got[:, slice_width].astype(jnp.int32) * 128 + got[:, slice_width + 1].astype(jnp.int32) - 1
    )
    in_sum = scatter_items(got[:, :slice_width], targets, new_count)
    select = select_rows(new_mask, new_count)
    params = jnp.dot(select, table, preferred_element_type=jnp.float32)
    partial_raw = lax.dot_general(
        spread, table, (((1,), (1,)), ((), ())), preferred_element_type=jnp.float32
    ).astype(jnp.bfloat16)
    raw = lax.psum_scatter(partial_raw, "dp", scatter_dimension=0, tiled=True)
    loss, error = softmax_error(raw.astype(jnp.float32), labels.reshape(-1), vocab_start)
    piece = lax.all_gather(error, "dp", axis=0, tiled=True)
    part = jnp.dot(piece, table, preferred_element_type=jnp.float32)
    d_hidden = finish_hidden(part, groups, shards)
    chosen = lax.dot_general(
        piece, select, (((1,), (1,)), ((), ())), preferred_element_type=jnp.float32
    ).astype(jnp.bfloat16)
    grads = in_sum + lax.dot_general(
        chosen, spread, (((0,), (0,)), ((), ())), preferred_element_type=jnp.float32
    )
    first_out = beta_one * first_moment + (1.0 - beta_one) * grads
    second_out = beta_two * second_moment + (1.0 - beta_two) * grads * grads
    update = (
        first_out
        / (1.0 - beta_one**step_count)
        / (jnp.sqrt(second_out / (1.0 - beta_two**step_count)) + epsilon)
        + decay_rate * params
    )
    return (
        loss.reshape(1, blocks, span),
        d_hidden.reshape(1, blocks, span, -1),
        update,
        first_out,
        second_out,
    )


def solution(mesh):
    return jax.shard_map(
        body,
        mesh=mesh,
        in_specs=(
            P("dp", None, None, None),
            P("vocab", "dp"),
            P("vocab"),
            P("dp", None, None),
            P("dp", None, "vocab", None),
            P("dp", None, "vocab", None),
            P("dp", None, "vocab"),
            P("vocab", "dp"),
            P("vocab", "dp"),
        ),
        out_specs=(
            P("dp", None, None),
            P("dp", None, None, "vocab"),
            P("vocab", "dp"),
            P("vocab", "dp"),
            P("vocab", "dp"),
        ),
        check_vma=False,
    )
```

```python
import functools

import jax
import jax.numpy as jnp
from jax import lax
from jax.experimental import pallas as pl
from jax.experimental.pallas import tpu as pltpu
from jax.sharding import PartitionSpec as P

cap_value = 30.0
beta_one = 0.9
beta_two = 0.95
step_count = 10
epsilon = 1e-08
decay_rate = 0.1


def select_rows(new_mask, new_count):
    ranked = jnp.cumsum(new_mask) - 1
    wanted = (ranked[None, :] == jnp.arange(new_count, dtype=jnp.int32)[:, None]) & (
        new_mask[None, :] == 1
    )
    return wanted.astype(jnp.bfloat16)


MESH = pl.DeviceIdType.MESH


def error_kernel(
    groups,
    shards,
    raw_ref,
    label_ref,
    table_ref,
    loss_ref,
    piece_ref,
    sum_ref,
    stats,
    square,
    part,
    inbox,
    stat_send,
    stat_recv,
    line_send,
    line_recv,
    sum_send,
    sum_recv,
):
    z = lax.axis_index("dp")
    me = lax.axis_index("vocab")
    tokens, rows_here = raw_ref.shape
    chunk_rows = sum_ref.shape[0]
    ratio = shards // groups
    halves = 2
    half = tokens // halves

    barrier = pltpu.get_barrier_semaphore()
    for k in range(1, shards):
        pl.semaphore_signal(
            barrier, inc=1, device_id={"vocab": lax.rem(me + k, shards)}, device_id_type=MESH
        )

    @pl.when(z < groups - 1)
    def _():
        pl.semaphore_signal(barrier, inc=1, device_id={"dp": z + 1}, device_id_type=MESH)

    @pl.when(z > 0)
    def _():
        pl.semaphore_signal(barrier, inc=1, device_id={"dp": z - 1}, device_id_type=MESH)

    capped = cap_value * jnp.tanh(raw_ref[...].astype(jnp.float32) / cap_value)
    expd = jnp.exp(capped)
    ids = lax.broadcasted_iota(jnp.int32, (tokens, rows_here), 1) + me * rows_here
    hits = ids == label_ref[...]
    local_total = jnp.sum(expd, axis=1, keepdims=True)
    local_pick = jnp.sum(jnp.where(hits, capped, 0.0), axis=1, keepdims=True)
    lane = lax.broadcasted_iota(jnp.int32, (tokens, 128), 1)
    square[...] = jnp.where(lane == 0, local_total, jnp.where(lane == 1, local_pick, 0.0)).T
    stats[0] = square[0:8, :]

    near = (z < groups - 1).astype(jnp.int32) + (z > 0).astype(jnp.int32)
    pl.semaphore_wait(barrier, shards - 1 + near)

    def stat_copy(k):
        return pltpu.make_async_remote_copy(
            src_ref=stats.at[0],
            dst_ref=stats.at[k],
            send_sem=stat_send.at[k],
            recv_sem=stat_recv.at[k],
            device_id={"vocab": lax.rem(me + k, shards)},
            device_id_type=MESH,
        )

    for k in range(1, shards):
        stat_copy(k).start()
    gathered = stats[0]
    for k in range(1, shards):
        stat_copy(k).wait_recv()
        gathered = gathered + stats[k]
    square[0:8, :] = gathered
    columns = square[...].T
    total = columns[:, 0:1]
    loss_ref[...] = jnp.log(total) - columns[:, 1:2]
    error = (expd / total - hits.astype(jnp.float32)) * (1.0 - (capped / cap_value) ** 2)
    piece_ref[z] = error.astype(jnp.bfloat16)
    for k in range(1, shards):
        stat_copy(k).wait_send()

    def line_copy(way, s, p, block, target):
        place = piece_ref.at[block, pl.ds(p * half, half)]
        return pltpu.make_async_remote_copy(
            src_ref=place,
            dst_ref=place,
            send_sem=line_send.at[way, s, p],
            recv_sem=line_recv.at[way, s, p],
            device_id={"dp": target},
            device_id_type=MESH,
        )

    def held(way, s):
        return (z - s, z - s >= 0) if way == 0 else (z + s, z + s < groups)

    def onward(way):
        return (z + 1, z < groups - 1) if way == 0 else (z - 1, z > 0)

    def sum_copy(chunk):
        return pltpu.make_async_remote_copy(
            src_ref=part.at[chunk],
            dst_ref=inbox.at[me],
            send_sem=sum_send.at[chunk],
            recv_sem=sum_recv.at[me],
            device_id={"vocab": chunk},
            device_id_type=MESH,
        )

    for s in range(groups):
        for p in range(halves):
            for way in range(2):
                block, have = held(way, s)
                target, more = onward(way)
                if s > 0:

                    @pl.when(have)
                    def _(way=way, s=s, p=p, block=block):
                        line_copy(way, s - 1, p, block, z).wait_recv()

                if s < groups - 1:

                    @pl.when(have & more)
                    def _(way=way, s=s, p=p, block=block, target=target):
                        line_copy(way, s, p, block, target).start()

        @pl.loop(0, 1 if s == 0 else 2)
        def _(way, s=s):
            block = z + s * (2 * way - 1)

            @pl.when((block >= 0) & (block < groups))
            def _():
                product = jnp.dot(
                    piece_ref[block], table_ref[...], preferred_element_type=jnp.float32
                ).astype(jnp.bfloat16)
                for b in range(ratio):
                    chunk = block * ratio + b
                    part[chunk] = product[b * chunk_rows : (b + 1) * chunk_rows]

                    @pl.when(chunk != me)
                    def _(chunk=chunk):
                        sum_copy(chunk).start()

    summed = part[me].astype(jnp.float32)
    for k in range(1, shards):
        source = lax.rem(me + k, shards)
        pltpu.make_async_remote_copy(
            src_ref=part.at[source],
            dst_ref=inbox.at[source],
            send_sem=sum_send.at[source],
            recv_sem=sum_recv.at[source],
            device_id={"vocab": source},
            device_id_type=MESH,
        ).wait()
        summed = summed + inbox[source].astype(jnp.float32)
    sum_ref[...] = summed.astype(jnp.bfloat16)
    for s in range(groups - 1):
        for p in range(halves):
            for way in range(2):
                block, have = held(way, s)
                target, more = onward(way)

                @pl.when(have & more)
                def _(way=way, s=s, p=p, block=block, target=target):
                    line_copy(way, s, p, block, target).wait_send()


def error_and_sums(raw, labels, table, groups, shards):
    tokens, rows_here = raw.shape
    slice_width = table.shape[1]
    chunk_rows = groups * tokens // shards
    vmem = pl.BlockSpec(memory_space=pltpu.VMEM)
    return pl.pallas_call(
        functools.partial(error_kernel, groups, shards),
        out_shape=(
            jax.ShapeDtypeStruct((tokens, 1), jnp.float32),
            jax.ShapeDtypeStruct((groups, tokens, rows_here), jnp.bfloat16),
            jax.ShapeDtypeStruct((chunk_rows, slice_width), jnp.bfloat16),
        ),
        in_specs=[vmem] * 3,
        out_specs=(vmem,) * 3,
        scratch_shapes=[
            pltpu.VMEM((shards, 8, tokens), jnp.float32),
            pltpu.VMEM((128, tokens), jnp.float32),
            pltpu.VMEM((shards, chunk_rows, slice_width), jnp.bfloat16),
            pltpu.VMEM((shards, chunk_rows, slice_width), jnp.bfloat16),
            pltpu.SemaphoreType.DMA((shards,)),
            pltpu.SemaphoreType.DMA((shards,)),
            pltpu.SemaphoreType.DMA((2, groups, 2)),
            pltpu.SemaphoreType.DMA((2, groups, 2)),
            pltpu.SemaphoreType.DMA((shards,)),
            pltpu.SemaphoreType.DMA((shards,)),
        ],
        compiler_params=pltpu.CompilerParams(
            collective_id=0, has_side_effects=True, vmem_limit_bytes=48 * 1024 * 1024
        ),
    )(raw, labels, table)


def gather_states(states, shards):
    share = states.shape[0] // shards
    mine = lax.dynamic_slice_in_dim(states, lax.axis_index("vocab") * share, share, 0)
    groups = lax.axis_size("dp")
    cut = lax.all_to_all(mine, "dp", split_axis=1, concat_axis=0, tiled=True)
    cut = cut.reshape(groups, share, -1)
    return lax.all_gather(cut, "vocab", axis=1, tiled=True).reshape(groups * share * shards, -1)


def finish_hidden(mine, groups, shards):
    ratio = shards // groups
    rows, columns = mine.shape
    pieces = mine.reshape(rows, ratio, columns // ratio).transpose(1, 0, 2)
    place = lax.rem(lax.axis_index("vocab"), ratio)
    got = []
    for r in range(ratio):
        pairs = [
            (d * shards + v, (v // ratio) * shards + ratio * d + (v % ratio + r) % ratio)
            for d in range(groups)
            for v in range(shards)
        ]
        piece = lax.dynamic_index_in_dim(pieces, lax.rem(place + r, ratio), 0, keepdims=False)
        got.append(lax.ppermute(piece, ("dp", "vocab"), pairs))
    order = lax.rem(place - jnp.arange(ratio, dtype=jnp.int32) + ratio, ratio)
    return jnp.stack(got)[order].reshape(ratio * rows, columns // ratio)


def pack_items(rows, owner, slot, shards, capacity, groups):
    onehot = (owner[:, None] == jnp.arange(shards, dtype=jnp.int32)[None, :]).astype(jnp.int32)
    running = jnp.cumsum(onehot, axis=0)
    ranked = jnp.sum(onehot * running, axis=1) - 1
    place = owner * capacity + ranked
    placing = jnp.arange(shards * capacity, dtype=jnp.int32)[:, None] == place[None, :]
    sent = jnp.dot(placing.astype(jnp.bfloat16), rows, preferred_element_type=jnp.float32).astype(
        jnp.bfloat16
    )
    targets = jnp.sum(placing.astype(jnp.int32) * (slot + 1)[None, :], axis=1)
    sent = sent.reshape(shards, capacity, groups, -1).transpose(2, 0, 1, 3)
    high, low = (targets // 128).astype(jnp.bfloat16), (targets % 128).astype(jnp.bfloat16)
    code = jnp.stack([high, low], axis=1).reshape(1, shards, capacity, 2)
    code = jnp.broadcast_to(jnp.pad(code, ((0, 0), (0, 0), (0, 0), (0, 126))), (groups, shards, capacity, 128))
    return jnp.concatenate([sent, code], axis=3)


def scatter_items(rows, targets, new_count):
    picking = (jnp.arange(new_count, dtype=jnp.int32)[:, None] == targets[None, :]).astype(
        jnp.bfloat16
    )
    return jnp.dot(picking, rows, preferred_element_type=jnp.float32)


def body(
    hidden, table, new_mask, labels, in_grad, item_owner, item_slot, first_moment, second_moment
):
    blocks, span, width = hidden.shape[1:]
    slice_width = table.shape[1]
    new_count = first_moment.shape[0]
    shards = lax.axis_size("vocab")
    groups = lax.axis_size("dp")
    items_here = in_grad.shape[2]
    capacity = max(2, (2 * items_here + shards - 1) // shards)
    spread = gather_states(hidden.reshape(blocks * span, width), shards)
    packed = jnp.concatenate(
        [
            pack_items(
                in_grad[0, c], item_owner[0, c, :, 0], item_slot[0, c], shards, capacity, groups
            )
            for c in range(blocks)
        ],
        axis=2,
    ).reshape(groups * shards, blocks * capacity, slice_width + 128)
    got = lax.all_to_all(packed, ("dp", "vocab"), split_axis=0, concat_axis=0, tiled=True)
    got = got.reshape(-1, slice_width + 128)
    select = select_rows(new_mask, new_count)
    params = jnp.dot(select, table, preferred_element_type=jnp.float32)
    partial_raw = lax.dot_general(
        spread, table, (((1,), (1,)), ((), ())), preferred_element_type=jnp.float32
    ).astype(jnp.bfloat16)
    partial_raw, got = lax.optimization_barrier((partial_raw, got))
    raw = lax.psum_scatter(partial_raw, "dp", scatter_dimension=0, tiled=True)
    loss, piece, summed = error_and_sums(raw, labels.reshape(-1, 1), table, groups, shards)
    piece = piece.reshape(-1, piece.shape[2])
    d_hidden = finish_hidden(summed, groups, shards)
    targets = (
        got[:, slice_width].astype(jnp.int32) * 128 + got[:, slice_width + 1].astype(jnp.int32) - 1
    )
    in_sum = scatter_items(got[:, :slice_width], targets, new_count)
    chosen = lax.dot_general(
        piece, select, (((1,), (1,)), ((), ())), preferred_element_type=jnp.float32
    ).astype(jnp.bfloat16)
    grads = in_sum + lax.dot_general(
        chosen, spread, (((0,), (0,)), ((), ())), preferred_element_type=jnp.float32
    )
    first_out = beta_one * first_moment + (1.0 - beta_one) * grads
    second_out = beta_two * second_moment + (1.0 - beta_two) * grads * grads
    update = (
        first_out
        / (1.0 - beta_one**step_count)
        / (jnp.sqrt(second_out / (1.0 - beta_two**step_count)) + epsilon)
        + decay_rate * params
    )
    return (
        loss.reshape(1, blocks, span),
        d_hidden.reshape(1, blocks, span, -1),
        update,
        first_out,
        second_out,
    )


def solution(mesh):
    return jax.shard_map(
        body,
        mesh=mesh,
        in_specs=(
            P("dp", None, None, None),
            P("vocab", "dp"),
            P("vocab"),
            P("dp", None, None),
            P("dp", None, "vocab", None),
            P("dp", None, "vocab", None),
            P("dp", None, "vocab"),
            P("vocab", "dp"),
            P("vocab", "dp"),
        ),
        out_specs=(
            P("dp", None, None),
            P("dp", None, None, "vocab"),
            P("vocab", "dp"),
            P("vocab", "dp"),
            P("vocab", "dp"),
        ),
        check_vma=False,
    )
```

```python
import functools

import jax
import jax.numpy as jnp
from jax import lax
from jax.experimental import pallas as pl
from jax.experimental.pallas import tpu as pltpu
from jax.sharding import PartitionSpec as P

cap_value = 30.0
beta_one = 0.9
beta_two = 0.95
step_count = 10
epsilon = 1e-08
decay_rate = 0.1


def select_rows(new_mask, new_count):
    ranked = jnp.cumsum(new_mask) - 1
    wanted = (ranked[None, :] == jnp.arange(new_count, dtype=jnp.int32)[:, None]) & (
        new_mask[None, :] == 1
    )
    return wanted.astype(jnp.bfloat16)


MESH = pl.DeviceIdType.MESH


def error_kernel(
    groups,
    shards,
    raw_ref,
    label_ref,
    table_ref,
    packed_ref,
    loss_ref,
    piece_ref,
    sum_ref,
    got_ref,
    stats,
    square,
    part,
    inbox,
    stat_send,
    stat_recv,
    line_send,
    line_recv,
    sum_send,
    sum_recv,
    item_send,
    item_recv,
):
    z = lax.axis_index("dp")
    me = lax.axis_index("vocab")
    tokens, rows_here = raw_ref.shape
    chunk_rows = sum_ref.shape[0]
    ratio = shards // groups
    halves = 2
    half = tokens // halves

    barrier = pltpu.get_barrier_semaphore()
    for k in range(1, shards):
        pl.semaphore_signal(
            barrier, inc=1, device_id={"vocab": lax.rem(me + k, shards)}, device_id_type=MESH
        )

    @pl.when(z < groups - 1)
    def _():
        pl.semaphore_signal(barrier, inc=1, device_id={"dp": z + 1}, device_id_type=MESH)

    @pl.when(z > 0)
    def _():
        pl.semaphore_signal(barrier, inc=1, device_id={"dp": z - 1}, device_id_type=MESH)

    capped = cap_value * jnp.tanh(raw_ref[...].astype(jnp.float32) / cap_value)
    expd = jnp.exp(capped)
    ids = lax.broadcasted_iota(jnp.int32, (tokens, rows_here), 1) + me * rows_here
    hits = ids == label_ref[...]
    local_total = jnp.sum(expd, axis=1, keepdims=True)
    local_pick = jnp.sum(jnp.where(hits, capped, 0.0), axis=1, keepdims=True)
    lane = lax.broadcasted_iota(jnp.int32, (tokens, 128), 1)
    square[...] = jnp.where(lane == 0, local_total, jnp.where(lane == 1, local_pick, 0.0)).T
    stats[0] = square[0:8, :]

    near = (z < groups - 1).astype(jnp.int32) + (z > 0).astype(jnp.int32)
    pl.semaphore_wait(barrier, shards - 1 + near)

    def stat_copy(k):
        return pltpu.make_async_remote_copy(
            src_ref=stats.at[0],
            dst_ref=stats.at[k],
            send_sem=stat_send.at[k],
            recv_sem=stat_recv.at[k],
            device_id={"vocab": lax.rem(me + k, shards)},
            device_id_type=MESH,
        )

    for k in range(1, shards):
        stat_copy(k).start()

    def item_copy(k):
        target = lax.rem(me + k, shards)
        return pltpu.make_async_remote_copy(
            src_ref=packed_ref.at[target],
            dst_ref=got_ref.at[me],
            send_sem=item_send.at[k],
            recv_sem=item_recv.at[k],
            device_id={"vocab": target},
            device_id_type=MESH,
        )

    gathered = stats[0]
    for k in range(1, shards):
        stat_copy(k).wait_recv()
        gathered = gathered + stats[k]
    square[0:8, :] = gathered
    columns = square[...].T
    total = columns[:, 0:1]
    loss_ref[...] = jnp.log(total) - columns[:, 1:2]
    error = (expd / total - hits.astype(jnp.float32)) * (1.0 - (capped / cap_value) ** 2)
    piece_ref[z] = error.astype(jnp.bfloat16)
    for k in range(1, shards):
        stat_copy(k).wait_send()

    for k in range(1, shards):
        item_copy(k).start()
    got_ref[me] = packed_ref[me]

    def line_copy(way, s, p, block, target):
        place = piece_ref.at[block, pl.ds(p * half, half)]
        return pltpu.make_async_remote_copy(
            src_ref=place,
            dst_ref=place,
            send_sem=line_send.at[way, s, p],
            recv_sem=line_recv.at[way, s, p],
            device_id={"dp": target},
            device_id_type=MESH,
        )

    def held(way, s):
        return (z - s, z - s >= 0) if way == 0 else (z + s, z + s < groups)

    def onward(way):
        return (z + 1, z < groups - 1) if way == 0 else (z - 1, z > 0)

    def sum_copy(chunk):
        return pltpu.make_async_remote_copy(
            src_ref=part.at[chunk],
            dst_ref=inbox.at[me],
            send_sem=sum_send.at[chunk],
            recv_sem=sum_recv.at[me],
            device_id={"vocab": chunk},
            device_id_type=MESH,
        )

    for s in range(groups):
        for p in range(halves):
            for way in range(2):
                block, have = held(way, s)
                target, more = onward(way)
                if s > 0:

                    @pl.when(have)
                    def _(way=way, s=s, p=p, block=block):
                        line_copy(way, s - 1, p, block, z).wait_recv()

                if s < groups - 1:

                    @pl.when(have & more)
                    def _(way=way, s=s, p=p, block=block, target=target):
                        line_copy(way, s, p, block, target).start()

        @pl.loop(0, 1 if s == 0 else 2)
        def _(way, s=s):
            block = z + s * (2 * way - 1)

            @pl.when((block >= 0) & (block < groups))
            def _():
                product = jnp.dot(
                    piece_ref[block], table_ref[...], preferred_element_type=jnp.float32
                ).astype(jnp.bfloat16)
                for b in range(ratio):
                    chunk = block * ratio + b
                    part[chunk] = product[b * chunk_rows : (b + 1) * chunk_rows]

                    @pl.when(chunk != me)
                    def _(chunk=chunk):
                        sum_copy(chunk).start()

    summed = part[me].astype(jnp.float32)
    for k in range(1, shards):
        source = lax.rem(me + k, shards)
        pltpu.make_async_remote_copy(
            src_ref=part.at[source],
            dst_ref=inbox.at[source],
            send_sem=sum_send.at[source],
            recv_sem=sum_recv.at[source],
            device_id={"vocab": source},
            device_id_type=MESH,
        ).wait()
        summed = summed + inbox[source].astype(jnp.float32)
    sum_ref[...] = summed.astype(jnp.bfloat16)
    for k in range(1, shards):
        item_copy(k).wait()
    for s in range(groups - 1):
        for p in range(halves):
            for way in range(2):
                block, have = held(way, s)
                target, more = onward(way)

                @pl.when(have & more)
                def _(way=way, s=s, p=p, block=block, target=target):
                    line_copy(way, s, p, block, target).wait_send()


def error_and_sums(raw, labels, table, packed, groups, shards):
    tokens, rows_here = raw.shape
    slice_width = table.shape[1]
    chunk_rows = groups * tokens // shards
    vmem = pl.BlockSpec(memory_space=pltpu.VMEM)
    return pl.pallas_call(
        functools.partial(error_kernel, groups, shards),
        out_shape=(
            jax.ShapeDtypeStruct((tokens, 1), jnp.float32),
            jax.ShapeDtypeStruct((groups, tokens, rows_here), jnp.bfloat16),
            jax.ShapeDtypeStruct((chunk_rows, slice_width), jnp.bfloat16),
            jax.ShapeDtypeStruct(packed.shape, packed.dtype),
        ),
        in_specs=[vmem] * 4,
        out_specs=(vmem,) * 4,
        scratch_shapes=[
            pltpu.VMEM((shards, 8, tokens), jnp.float32),
            pltpu.VMEM((128, tokens), jnp.float32),
            pltpu.VMEM((shards, chunk_rows, slice_width), jnp.bfloat16),
            pltpu.VMEM((shards, chunk_rows, slice_width), jnp.bfloat16),
            pltpu.SemaphoreType.DMA((shards,)),
            pltpu.SemaphoreType.DMA((shards,)),
            pltpu.SemaphoreType.DMA((2, groups, 2)),
            pltpu.SemaphoreType.DMA((2, groups, 2)),
            pltpu.SemaphoreType.DMA((shards,)),
            pltpu.SemaphoreType.DMA((shards,)),
            pltpu.SemaphoreType.DMA((shards,)),
            pltpu.SemaphoreType.DMA((shards,)),
        ],
        compiler_params=pltpu.CompilerParams(
            collective_id=0, has_side_effects=True, vmem_limit_bytes=48 * 1024 * 1024
        ),
    )(raw, labels, table, packed)


def spread_kernel(
    groups,
    shards,
    mine_ref,
    items_ref,
    out_ref,
    got_ref,
    cut_send,
    cut_recv,
    item_send,
    item_recv,
    plane_send,
    plane_recv,
):
    z = lax.axis_index("dp")
    me = lax.axis_index("vocab")
    barrier = pltpu.get_barrier_semaphore()
    for k in range(1, shards):
        pl.semaphore_signal(
            barrier, inc=1, device_id={"vocab": lax.rem(me + k, shards)}, device_id_type=MESH
        )
    for j in range(1, groups):
        pl.semaphore_signal(
            barrier, inc=1, device_id={"dp": lax.rem(z + j, groups)}, device_id_type=MESH
        )
    pl.semaphore_wait(barrier, shards + groups - 2)

    def cut_copy(j):
        target = lax.rem(z + j, groups)
        return pltpu.make_async_remote_copy(
            src_ref=mine_ref.at[target],
            dst_ref=out_ref.at[me, z],
            send_sem=cut_send.at[j],
            recv_sem=cut_recv.at[j],
            device_id={"dp": target},
            device_id_type=MESH,
        )

    def item_copy(j):
        target = lax.rem(z + j, groups)
        return pltpu.make_async_remote_copy(
            src_ref=items_ref.at[target],
            dst_ref=got_ref.at[z],
            send_sem=item_send.at[j],
            recv_sem=item_recv.at[j],
            device_id={"dp": target},
            device_id_type=MESH,
        )

    def plane_copy(j, k):
        place = out_ref.at[me, lax.rem(z + groups - j, groups)]
        return pltpu.make_async_remote_copy(
            src_ref=place,
            dst_ref=place,
            send_sem=plane_send.at[j, k],
            recv_sem=plane_recv.at[j, k],
            device_id={"vocab": lax.rem(me + k, shards)},
            device_id_type=MESH,
        )

    for j in range(1, groups):
        cut_copy(j).start()
    for j in range(1, groups):
        item_copy(j).start()
    out_ref[me, z] = mine_ref[z]
    got_ref[z] = items_ref[z]
    for j in range(groups):
        if j > 0:
            cut_copy(j).wait_recv()
        for k in range(1, shards):
            plane_copy(j, k).start()
    for j in range(groups):
        for k in range(1, shards):
            plane_copy(j, k).wait()
    for j in range(1, groups):
        cut_copy(j).wait_send()
        item_copy(j).wait()


def spread_states(states, items, groups, shards):
    share = states.shape[0] // shards
    mine = lax.dynamic_slice_in_dim(states, lax.axis_index("vocab") * share, share, 0)
    mine = mine.reshape(share, groups, -1).transpose(1, 0, 2)
    vmem = pl.BlockSpec(memory_space=pltpu.VMEM)
    dma = pltpu.SemaphoreType.DMA
    spread, got = pl.pallas_call(
        functools.partial(spread_kernel, groups, shards),
        out_shape=(
            jax.ShapeDtypeStruct((shards,) + mine.shape, mine.dtype),
            jax.ShapeDtypeStruct(items.shape, items.dtype),
        ),
        in_specs=[vmem] * 2,
        out_specs=(vmem,) * 2,
        scratch_shapes=[
            dma((groups,)),
            dma((groups,)),
            dma((groups,)),
            dma((groups,)),
            dma((groups, shards)),
            dma((groups, shards)),
        ],
        compiler_params=pltpu.CompilerParams(
            collective_id=1, has_side_effects=True, vmem_limit_bytes=24 * 1024 * 1024
        ),
    )(mine, items)
    spread = spread.transpose(1, 0, 2, 3).reshape(groups * share * shards, -1)
    return spread, got.reshape(-1, items.shape[2])


def finish_hidden(mine, groups, shards):
    ratio = shards // groups
    rows, columns = mine.shape
    pieces = mine.reshape(rows, ratio, columns // ratio).transpose(1, 0, 2)
    place = lax.rem(lax.axis_index("vocab"), ratio)
    got = []
    for r in range(ratio):
        pairs = [
            (d * shards + v, (v // ratio) * shards + ratio * d + (v % ratio + r) % ratio)
            for d in range(groups)
            for v in range(shards)
        ]
        piece = lax.dynamic_index_in_dim(pieces, lax.rem(place + r, ratio), 0, keepdims=False)
        got.append(lax.ppermute(piece, ("dp", "vocab"), pairs))
    order = lax.rem(place - jnp.arange(ratio, dtype=jnp.int32) + ratio, ratio)
    return jnp.stack(got)[order].reshape(ratio * rows, columns // ratio)


def code_items(rows, owner, slot, groups):
    mark = slot + 1
    code = jnp.stack([owner, mark // 128, mark % 128], axis=1).astype(jnp.bfloat16)
    code = jnp.broadcast_to(jnp.pad(code, ((0, 0), (0, 125))), (groups, rows.shape[0], 128))
    cut = rows.reshape(rows.shape[0], groups, -1).transpose(1, 0, 2)
    return jnp.concatenate([cut, code], axis=2)


def pack_items(items, slice_width, shards, capacity):
    owner = items[:, slice_width].astype(jnp.int32)
    onehot = (owner[:, None] == jnp.arange(shards, dtype=jnp.int32)[None, :]).astype(jnp.int32)
    ranked = jnp.sum(onehot * jnp.cumsum(onehot, axis=0), axis=1) - 1
    place = owner * capacity + ranked
    placing = jnp.arange(shards * capacity, dtype=jnp.int32)[:, None] == place[None, :]
    packed = jnp.dot(placing.astype(jnp.bfloat16), items, preferred_element_type=jnp.float32)
    return packed.astype(jnp.bfloat16).reshape(shards, capacity, -1)


def scatter_items(rows, targets, new_count):
    picking = (jnp.arange(new_count, dtype=jnp.int32)[:, None] == targets[None, :]).astype(
        jnp.bfloat16
    )
    return jnp.dot(picking, rows, preferred_element_type=jnp.float32)


def body(
    hidden, table, new_mask, labels, in_grad, item_owner, item_slot, first_moment, second_moment
):
    blocks, span, width = hidden.shape[1:]
    slice_width = table.shape[1]
    new_count = first_moment.shape[0]
    shards = lax.axis_size("vocab")
    groups = lax.axis_size("dp")
    items_here = in_grad.shape[2]
    capacity = max(2, (2 * items_here + shards - 1) // shards)
    coded = code_items(
        in_grad.reshape(blocks * items_here, width),
        item_owner.reshape(-1),
        item_slot.reshape(-1),
        groups,
    )
    spread, items = spread_states(hidden.reshape(blocks * span, width), coded, groups, shards)
    packed = pack_items(items, slice_width, shards, groups * blocks * capacity)
    select = select_rows(new_mask, new_count)
    params = jnp.dot(select, table, preferred_element_type=jnp.float32)
    partial_raw = lax.dot_general(
        spread, table, (((1,), (1,)), ((), ())), preferred_element_type=jnp.float32
    ).astype(jnp.bfloat16)
    raw = lax.psum_scatter(partial_raw, "dp", scatter_dimension=0, tiled=True)
    raw, packed, params = lax.optimization_barrier((raw, packed, params))
    loss, piece, summed, got = error_and_sums(
        raw, labels.reshape(-1, 1), table, packed, groups, shards
    )
    got = got.reshape(-1, got.shape[2])
    piece = piece.reshape(-1, piece.shape[2])
    d_hidden = finish_hidden(summed, groups, shards)
    targets = (
        got[:, slice_width + 1].astype(jnp.int32) * 128
        + got[:, slice_width + 2].astype(jnp.int32)
        - 1
    )
    in_sum = scatter_items(got[:, :slice_width], targets, new_count)
    chosen = lax.dot_general(
        piece, select, (((1,), (1,)), ((), ())), preferred_element_type=jnp.float32
    ).astype(jnp.bfloat16)
    grads = in_sum + lax.dot_general(
        chosen, spread, (((0,), (0,)), ((), ())), preferred_element_type=jnp.float32
    )
    first_out = beta_one * first_moment + (1.0 - beta_one) * grads
    second_out = beta_two * second_moment + (1.0 - beta_two) * grads * grads
    update = (
        first_out
        / (1.0 - beta_one**step_count)
        / (jnp.sqrt(second_out / (1.0 - beta_two**step_count)) + epsilon)
        + decay_rate * params
    )
    return (
        loss.reshape(1, blocks, span),
        d_hidden.reshape(1, blocks, span, -1),
        update,
        first_out,
        second_out,
    )


def solution(mesh):
    return jax.shard_map(
        body,
        mesh=mesh,
        in_specs=(
            P("dp", None, None, None),
            P("vocab", "dp"),
            P("vocab"),
            P("dp", None, None),
            P("dp", None, "vocab", None),
            P("dp", None, "vocab", None),
            P("dp", None, "vocab"),
            P("vocab", "dp"),
            P("vocab", "dp"),
        ),
        out_specs=(
            P("dp", None, None),
            P("dp", None, None, "vocab"),
            P("vocab", "dp"),
            P("vocab", "dp"),
            P("vocab", "dp"),
        ),
        check_vma=False,
    )
```

```python
import functools

import jax
import jax.numpy as jnp
from jax import lax
from jax.experimental import pallas as pl
from jax.experimental.pallas import tpu as pltpu
from jax.sharding import PartitionSpec as P

cap_value = 30.0
beta_one = 0.9
beta_two = 0.95
step_count = 10
epsilon = 1e-08
decay_rate = 0.1


def select_rows(new_mask, new_count):
    ranked = jnp.cumsum(new_mask) - 1
    wanted = (ranked[None, :] == jnp.arange(new_count, dtype=jnp.int32)[:, None]) & (
        new_mask[None, :] == 1
    )
    return wanted.astype(jnp.bfloat16)


MESH = pl.DeviceIdType.MESH


def error_kernel(
    groups,
    shards,
    spread_ref,
    label_ref,
    table_ref,
    packed_ref,
    select_ref,
    params_ref,
    loss_ref,
    piece_ref,
    sum_ref,
    got_ref,
    stats,
    square,
    part,
    inbox,
    stat_send,
    stat_recv,
    line_send,
    line_recv,
    sum_send,
    sum_recv,
    item_send,
    item_recv,
    outbox,
    logits_in,
    raw,
    chain_send,
    chain_recv,
):
    z = lax.axis_index("dp")
    me = lax.axis_index("vocab")
    tokens = spread_ref.shape[1]
    rows_here = table_ref.shape[0]
    chunk_rows = sum_ref.shape[0]
    ratio = shards // groups
    halves = 2
    half = tokens // halves

    barrier = pltpu.get_barrier_semaphore()
    for k in range(1, shards):
        pl.semaphore_signal(
            barrier, inc=1, device_id={"vocab": lax.rem(me + k, shards)}, device_id_type=MESH
        )

    @pl.when(z < groups - 1)
    def _():
        pl.semaphore_signal(barrier, inc=1, device_id={"dp": z + 1}, device_id_type=MESH)

    @pl.when(z > 0)
    def _():
        pl.semaphore_signal(barrier, inc=1, device_id={"dp": z - 1}, device_id_type=MESH)

    near = (z < groups - 1).astype(jnp.int32) + (z > 0).astype(jnp.int32)
    pl.semaphore_wait(barrier, shards - 1 + near)

    def partial_logits(block):
        return lax.dot_general(
            spread_ref[block],
            table_ref[...],
            (((1,), (1,)), ((), ())),
            preferred_element_type=jnp.float32,
        )

    def chain_copy(way, s):
        return pltpu.make_async_remote_copy(
            src_ref=outbox.at[way, s],
            dst_ref=logits_in.at[way, s],
            send_sem=chain_send.at[way, s],
            recv_sem=chain_recv.at[way, s],
            device_id={"dp": z + 1 - 2 * way},
            device_id_type=MESH,
        )

    for s in range(groups - 1):

        @pl.loop(0, 2)
        def _(i, s=s):
            way = lax.rem(i + (2 * z) // groups, 2)
            block = groups - 1 - s + way * (2 * s - groups + 1)

            @pl.when((block - z) * (1 - 2 * way) > 0)
            def _():
                raw[...] = partial_logits(block)

                @pl.when(z * (1 - way) + (groups - 1 - z) * way > 0)
                def _():
                    chain_copy(way, s).wait_recv()
                    raw[...] += logits_in[way, s].astype(jnp.float32)

                outbox[way, s] = raw[...].astype(jnp.bfloat16)
                chain_copy(way, s).start()

        if s == 0:
            params_ref[...] = jnp.dot(
                select_ref[...], table_ref[...], preferred_element_type=jnp.float32
            )

    raw[...] = partial_logits(z)

    @pl.when(z > 0)
    def _():
        chain_copy(0, groups - 1 - z).wait_recv()
        raw[...] += logits_in[0, groups - 1 - z].astype(jnp.float32)

    @pl.when(z < groups - 1)
    def _():
        chain_copy(1, z).wait_recv()
        raw[...] += logits_in[1, z].astype(jnp.float32)

    for s in range(groups - 1):

        @pl.loop(0, 2)
        def _(way, s=s):
            block = groups - 1 - s + way * (2 * s - groups + 1)

            @pl.when((block - z) * (1 - 2 * way) > 0)
            def _():
                chain_copy(way, s).wait_send()

    capped = cap_value * jnp.tanh(raw[...] / cap_value)
    expd = jnp.exp(capped)
    ids = lax.broadcasted_iota(jnp.int32, (tokens, rows_here), 1) + me * rows_here
    hits = ids == label_ref[...]
    local_total = jnp.sum(expd, axis=1, keepdims=True)
    local_pick = jnp.sum(jnp.where(hits, capped, 0.0), axis=1, keepdims=True)
    lane = lax.broadcasted_iota(jnp.int32, (tokens, 128), 1)
    square[...] = jnp.where(lane == 0, local_total, jnp.where(lane == 1, local_pick, 0.0)).T
    stats[0] = square[0:8, :]

    def stat_copy(k):
        return pltpu.make_async_remote_copy(
            src_ref=stats.at[0],
            dst_ref=stats.at[k],
            send_sem=stat_send.at[k],
            recv_sem=stat_recv.at[k],
            device_id={"vocab": lax.rem(me + k, shards)},
            device_id_type=MESH,
        )

    for k in range(1, shards):
        stat_copy(k).start()

    def item_copy(k):
        target = lax.rem(me + k, shards)
        return pltpu.make_async_remote_copy(
            src_ref=packed_ref.at[target],
            dst_ref=got_ref.at[me],
            send_sem=item_send.at[k],
            recv_sem=item_recv.at[k],
            device_id={"vocab": target},
            device_id_type=MESH,
        )

    gathered = stats[0]
    for k in range(1, shards):
        stat_copy(k).wait_recv()
        gathered = gathered + stats[k]
    square[0:8, :] = gathered
    columns = square[...].T
    total = columns[:, 0:1]
    loss_ref[...] = jnp.log(total) - columns[:, 1:2]
    error = (expd / total - hits.astype(jnp.float32)) * (1.0 - (capped / cap_value) ** 2)
    piece_ref[z] = error.astype(jnp.bfloat16)
    for k in range(1, shards):
        stat_copy(k).wait_send()

    for k in range(1, shards):
        item_copy(k).start()
    got_ref[me] = packed_ref[me]

    def line_copy(way, s, p, block, target):
        place = piece_ref.at[block, pl.ds(p * half, half)]
        return pltpu.make_async_remote_copy(
            src_ref=place,
            dst_ref=place,
            send_sem=line_send.at[way, s, p],
            recv_sem=line_recv.at[way, s, p],
            device_id={"dp": target},
            device_id_type=MESH,
        )

    def held(way, s):
        return (z - s, z - s >= 0) if way == 0 else (z + s, z + s < groups)

    def onward(way):
        return (z + 1, z < groups - 1) if way == 0 else (z - 1, z > 0)

    def sum_copy(chunk):
        return pltpu.make_async_remote_copy(
            src_ref=part.at[chunk],
            dst_ref=inbox.at[me],
            send_sem=sum_send.at[chunk],
            recv_sem=sum_recv.at[me],
            device_id={"vocab": chunk},
            device_id_type=MESH,
        )

    for s in range(groups):
        for p in range(halves):
            for way in range(2):
                block, have = held(way, s)
                target, more = onward(way)
                if s > 0:

                    @pl.when(have)
                    def _(way=way, s=s, p=p, block=block):
                        line_copy(way, s - 1, p, block, z).wait_recv()

                if s < groups - 1:

                    @pl.when(have & more)
                    def _(way=way, s=s, p=p, block=block, target=target):
                        line_copy(way, s, p, block, target).start()

        @pl.loop(0, 1 if s == 0 else 2)
        def _(way, s=s):
            block = z + s * (2 * way - 1)

            @pl.when((block >= 0) & (block < groups))
            def _():
                product = jnp.dot(
                    piece_ref[block], table_ref[...], preferred_element_type=jnp.float32
                ).astype(jnp.bfloat16)
                for b in range(ratio):
                    chunk = block * ratio + b
                    part[chunk] = product[b * chunk_rows : (b + 1) * chunk_rows]

                    @pl.when(chunk != me)
                    def _(chunk=chunk):
                        sum_copy(chunk).start()

    summed = part[me].astype(jnp.float32)
    for k in range(1, shards):
        source = lax.rem(me + k, shards)
        pltpu.make_async_remote_copy(
            src_ref=part.at[source],
            dst_ref=inbox.at[source],
            send_sem=sum_send.at[source],
            recv_sem=sum_recv.at[source],
            device_id={"vocab": source},
            device_id_type=MESH,
        ).wait()
        summed = summed + inbox[source].astype(jnp.float32)
    sum_ref[...] = summed.astype(jnp.bfloat16)
    for k in range(1, shards):
        item_copy(k).wait()
    for s in range(groups - 1):
        for p in range(halves):
            for way in range(2):
                block, have = held(way, s)
                target, more = onward(way)

                @pl.when(have & more)
                def _(way=way, s=s, p=p, block=block, target=target):
                    line_copy(way, s, p, block, target).wait_send()


def error_and_sums(spread, labels, table, packed, select, groups, shards):
    tokens, rows_here = spread.shape[1], table.shape[0]
    slice_width = table.shape[1]
    chunk_rows = groups * tokens // shards
    vmem = pl.BlockSpec(memory_space=pltpu.VMEM)
    return pl.pallas_call(
        functools.partial(error_kernel, groups, shards),
        out_shape=(
            jax.ShapeDtypeStruct((select.shape[0], slice_width), jnp.float32),
            jax.ShapeDtypeStruct((tokens, 1), jnp.float32),
            jax.ShapeDtypeStruct((groups, tokens, rows_here), jnp.bfloat16),
            jax.ShapeDtypeStruct((chunk_rows, slice_width), jnp.bfloat16),
            jax.ShapeDtypeStruct(packed.shape, packed.dtype),
        ),
        in_specs=[vmem] * 5,
        out_specs=(vmem,) * 5,
        scratch_shapes=[
            pltpu.VMEM((shards, 8, tokens), jnp.float32),
            pltpu.VMEM((128, tokens), jnp.float32),
            pltpu.VMEM((shards, chunk_rows, slice_width), jnp.bfloat16),
            pltpu.VMEM((shards, chunk_rows, slice_width), jnp.bfloat16),
            pltpu.SemaphoreType.DMA((shards,)),
            pltpu.SemaphoreType.DMA((shards,)),
            pltpu.SemaphoreType.DMA((2, groups, 2)),
            pltpu.SemaphoreType.DMA((2, groups, 2)),
            pltpu.SemaphoreType.DMA((shards,)),
            pltpu.SemaphoreType.DMA((shards,)),
            pltpu.SemaphoreType.DMA((shards,)),
            pltpu.SemaphoreType.DMA((shards,)),
            pltpu.VMEM((2, groups - 1, tokens, rows_here), jnp.bfloat16),
            pltpu.VMEM((2, groups - 1, tokens, rows_here), jnp.bfloat16),
            pltpu.VMEM((tokens, rows_here), jnp.float32),
            pltpu.SemaphoreType.DMA((2, groups)),
            pltpu.SemaphoreType.DMA((2, groups)),
        ],
        compiler_params=pltpu.CompilerParams(
            collective_id=0, has_side_effects=True, vmem_limit_bytes=58 * 1024 * 1024
        ),
    )(spread, labels, table, packed, select)


def spread_kernel(
    groups,
    shards,
    mine_ref,
    items_ref,
    out_ref,
    got_ref,
    cut_send,
    cut_recv,
    item_send,
    item_recv,
    plane_send,
    plane_recv,
):
    z = lax.axis_index("dp")
    me = lax.axis_index("vocab")
    barrier = pltpu.get_barrier_semaphore()
    for k in range(1, shards):
        pl.semaphore_signal(
            barrier, inc=1, device_id={"vocab": lax.rem(me + k, shards)}, device_id_type=MESH
        )
    for j in range(1, groups):
        pl.semaphore_signal(
            barrier, inc=1, device_id={"dp": lax.rem(z + j, groups)}, device_id_type=MESH
        )
    pl.semaphore_wait(barrier, shards + groups - 2)

    def cut_copy(j):
        target = lax.rem(z + j, groups)
        return pltpu.make_async_remote_copy(
            src_ref=mine_ref.at[target],
            dst_ref=out_ref.at[me, z],
            send_sem=cut_send.at[j],
            recv_sem=cut_recv.at[j],
            device_id={"dp": target},
            device_id_type=MESH,
        )

    def item_copy(j):
        target = lax.rem(z + j, groups)
        return pltpu.make_async_remote_copy(
            src_ref=items_ref.at[target],
            dst_ref=got_ref.at[z],
            send_sem=item_send.at[j],
            recv_sem=item_recv.at[j],
            device_id={"dp": target},
            device_id_type=MESH,
        )

    def plane_copy(j, k):
        place = out_ref.at[me, lax.rem(z + groups - j, groups)]
        return pltpu.make_async_remote_copy(
            src_ref=place,
            dst_ref=place,
            send_sem=plane_send.at[j, k],
            recv_sem=plane_recv.at[j, k],
            device_id={"vocab": lax.rem(me + k, shards)},
            device_id_type=MESH,
        )

    for j in range(1, groups):
        cut_copy(j).start()
    for j in range(1, groups):
        item_copy(j).start()
    out_ref[me, z] = mine_ref[z]
    got_ref[z] = items_ref[z]
    for j in range(groups):
        if j > 0:
            cut_copy(j).wait_recv()
        for k in range(1, shards):
            plane_copy(j, k).start()
    for j in range(groups):
        for k in range(1, shards):
            plane_copy(j, k).wait()
    for j in range(1, groups):
        cut_copy(j).wait_send()
        item_copy(j).wait()


def spread_states(states, items, groups, shards):
    share = states.shape[0] // shards
    mine = lax.dynamic_slice_in_dim(states, lax.axis_index("vocab") * share, share, 0)
    mine = mine.reshape(share, groups, -1).transpose(1, 0, 2)
    vmem = pl.BlockSpec(memory_space=pltpu.VMEM)
    dma = pltpu.SemaphoreType.DMA
    spread, got = pl.pallas_call(
        functools.partial(spread_kernel, groups, shards),
        out_shape=(
            jax.ShapeDtypeStruct((shards,) + mine.shape, mine.dtype),
            jax.ShapeDtypeStruct(items.shape, items.dtype),
        ),
        in_specs=[vmem] * 2,
        out_specs=(vmem,) * 2,
        scratch_shapes=[
            dma((groups,)),
            dma((groups,)),
            dma((groups,)),
            dma((groups,)),
            dma((groups, shards)),
            dma((groups, shards)),
        ],
        compiler_params=pltpu.CompilerParams(
            collective_id=1, has_side_effects=True, vmem_limit_bytes=24 * 1024 * 1024
        ),
    )(mine, items)
    spread = spread.transpose(1, 0, 2, 3).reshape(groups * share * shards, -1)
    return spread, got.reshape(-1, items.shape[2])


def finish_hidden(mine, groups, shards):
    ratio = shards // groups
    rows, columns = mine.shape
    pieces = mine.reshape(rows, ratio, columns // ratio).transpose(1, 0, 2)
    place = lax.rem(lax.axis_index("vocab"), ratio)
    got = []
    for r in range(ratio):
        pairs = [
            (d * shards + v, (v // ratio) * shards + ratio * d + (v % ratio + r) % ratio)
            for d in range(groups)
            for v in range(shards)
        ]
        piece = lax.dynamic_index_in_dim(pieces, lax.rem(place + r, ratio), 0, keepdims=False)
        got.append(lax.ppermute(piece, ("dp", "vocab"), pairs))
    order = lax.rem(place - jnp.arange(ratio, dtype=jnp.int32) + ratio, ratio)
    return jnp.stack(got)[order].reshape(ratio * rows, columns // ratio)


def code_items(rows, owner, slot, groups):
    mark = slot + 1
    code = jnp.stack([owner, mark // 128, mark % 128], axis=1).astype(jnp.bfloat16)
    code = jnp.broadcast_to(jnp.pad(code, ((0, 0), (0, 125))), (groups, rows.shape[0], 128))
    cut = rows.reshape(rows.shape[0], groups, -1).transpose(1, 0, 2)
    return jnp.concatenate([cut, code], axis=2)


def pack_items(items, slice_width, shards, capacity):
    owner = items[:, slice_width].astype(jnp.int32)
    onehot = (owner[:, None] == jnp.arange(shards, dtype=jnp.int32)[None, :]).astype(jnp.int32)
    ranked = jnp.sum(onehot * jnp.cumsum(onehot, axis=0), axis=1) - 1
    place = owner * capacity + ranked
    placing = jnp.arange(shards * capacity, dtype=jnp.int32)[:, None] == place[None, :]
    packed = jnp.dot(placing.astype(jnp.bfloat16), items, preferred_element_type=jnp.float32)
    return packed.astype(jnp.bfloat16).reshape(shards, capacity, -1)


def scatter_items(rows, targets, new_count):
    picking = (jnp.arange(new_count, dtype=jnp.int32)[:, None] == targets[None, :]).astype(
        jnp.bfloat16
    )
    return jnp.dot(picking, rows, preferred_element_type=jnp.float32)


def body(
    hidden, table, new_mask, labels, in_grad, item_owner, item_slot, first_moment, second_moment
):
    blocks, span, width = hidden.shape[1:]
    slice_width = table.shape[1]
    new_count = first_moment.shape[0]
    shards = lax.axis_size("vocab")
    groups = lax.axis_size("dp")
    items_here = in_grad.shape[2]
    capacity = max(2, (2 * items_here + shards - 1) // shards)
    coded = code_items(
        in_grad.reshape(blocks * items_here, width),
        item_owner.reshape(-1),
        item_slot.reshape(-1),
        groups,
    )
    spread, items = spread_states(hidden.reshape(blocks * span, width), coded, groups, shards)
    packed = pack_items(items, slice_width, shards, groups * blocks * capacity)
    select = select_rows(new_mask, new_count)
    params, loss, piece, summed, got = error_and_sums(
        spread.reshape(groups, blocks * span, slice_width),
        labels.reshape(-1, 1),
        table,
        packed,
        select,
        groups,
        shards,
    )
    got = got.reshape(-1, got.shape[2])
    piece = piece.reshape(-1, piece.shape[2])
    d_hidden = finish_hidden(summed, groups, shards)
    targets = (
        got[:, slice_width + 1].astype(jnp.int32) * 128
        + got[:, slice_width + 2].astype(jnp.int32)
        - 1
    )
    in_sum = scatter_items(got[:, :slice_width], targets, new_count)
    chosen = lax.dot_general(
        piece, select, (((1,), (1,)), ((), ())), preferred_element_type=jnp.float32
    ).astype(jnp.bfloat16)
    grads = in_sum + lax.dot_general(
        chosen, spread, (((0,), (0,)), ((), ())), preferred_element_type=jnp.float32
    )
    first_out = beta_one * first_moment + (1.0 - beta_one) * grads
    second_out = beta_two * second_moment + (1.0 - beta_two) * grads * grads
    update = (
        first_out
        / (1.0 - beta_one**step_count)
        / (jnp.sqrt(second_out / (1.0 - beta_two**step_count)) + epsilon)
        + decay_rate * params
    )
    return (
        loss.reshape(1, blocks, span),
        d_hidden.reshape(1, blocks, span, -1),
        update,
        first_out,
        second_out,
    )


def solution(mesh):
    return jax.shard_map(
        body,
        mesh=mesh,
        in_specs=(
            P("dp", None, None, None),
            P("vocab", "dp"),
            P("vocab"),
            P("dp", None, None),
            P("dp", None, "vocab", None),
            P("dp", None, "vocab", None),
            P("dp", None, "vocab"),
            P("vocab", "dp"),
            P("vocab", "dp"),
        ),
        out_specs=(
            P("dp", None, None),
            P("dp", None, None, "vocab"),
            P("vocab", "dp"),
            P("vocab", "dp"),
            P("vocab", "dp"),
        ),
        check_vma=False,
    )
```
